512 devices in a mesh: row: 32 (over z, x_lo), tensor: 8 (over y, x_hi), seq: 2 (over core).
Axes of the slice: x: 4 (x_hi: 2, x_lo: 2; x = x_hi * 2 + x_lo), y: 4, z: 16, core: 2. Of those that a mesh axis runs over, the one named last changes fastest.
Arguments:
- student: bfloat16 [8192, 5120], P(('seq', 'row'), 'tensor'), parts along dimension 0, may hold values from -6 to 6
- teacher: bfloat16 [8192, 8192], P(('seq', 'row'), 'tensor'), parts along dimension 0, may hold values from -6 to 6
- counts: int32 [6], P('seq'), parts along dimension 0, may hold values from 1 to 3072, 4096 in all
Outputs:
- gradient: bfloat16 [8192, 5120], P(('seq', 'row'), 'tensor'), parts along dimension 0
The draws below stay inside these ranges and needn't reach their ends.
There are 2 independent parts, one for each index of `seq`. The reference program is written for one: setup_inputs(seed, part) draws one part's arguments, and reference() takes and returns one part's arrays. A program takes and returns all parts, laid end to end along the dimension named above; each array names one. Nothing has to cross between parts.
Inputs may be any that keep to these rules, and one draw needn't show every extreme that they name: The counts sum to 4096; the largest is exactly 3072.
All inputs are finite; a program needn't handle non-finite values.
Results may differ from the reference program's by a relative error of at most 0.0049.
Values may be sent and summed in bfloat16 or wider, within the bound.
No kernel may reach another device: no remote copies, remote signals or barrier semaphores. Data moves between devices by JAX's collectives and lax.ppermute only.
A program may use at most 64 MiB of HBM per device.

```python
import math
import jax
import jax.numpy as jnp
import numpy as np
from jax import lax

DS = 5120
DT = 8192
SEQS = 3
ROWS = 4096


def steps_of(stream_key, dims, pieces, smallest, high):
    gain, own = 1.0, jax.random.fold_in(stream_key, 6)
    for axis_at, blocks in pieces:
        heights = jnp.exp(jax.random.uniform(jax.random.fold_in(own, axis_at), (blocks,), jnp.float32, smallest / len(pieces), high / len(pieces)))
        gain = gain * jnp.repeat(heights, dims[axis_at] // blocks).reshape([-1 if axis == axis_at else 1 for axis in range(len(dims))])
    return gain


def split_up(count, total, bound, skew):
    loads = [(1 << 20) // math.isqrt(standing ** skew) + 1 for standing in range(2, count + 1)]
    spare, given = total - bound - (count - 1), [1] * (count - 1)
    while spare > 0:
        movable = [i for i in range(count - 1) if given[i] < bound]
        mass, left = sum([loads[i] for i in movable]), spare
        for i in movable:
            extra = min(bound - given[i], max(1, left * loads[i] // mass), spare)
            given[i] = given[i] + extra
            spare = spare - extra
    return np.array([bound] + given)


def ragged(stream_key, count, total, bound, lean):
    if count == 2:
        one = jax.random.randint(stream_key, (), max(1, total - bound), min(bound, total - 1) + 1)
        return jnp.stack([one, total - one])
    sizes = jnp.asarray(split_up(count, total, bound, lean), jnp.int32)
    twos = (count - 1) // 2
    donor, receiver = sizes[1:1 + 2 * twos:2], sizes[2:2 + 2 * twos:2]
    margin = jnp.minimum(donor - 1, bound - receiver)
    moved = jax.random.randint(jax.random.fold_in(stream_key, 1), (twos,), 0, 1 << 20) % (margin + 1)
    sizes = sizes.at[1:1 + 2 * twos:2].set(donor - moved).at[2:2 + 2 * twos:2].set(receiver + moved)
    return sizes[jax.random.permutation(jax.random.fold_in(stream_key, 2), count)]


def bell_draw(key, shape, width, reach, shards=(), held_as=jnp.bfloat16):
    values = jax.random.normal(key, shape, jnp.float32) * width
    if len(shards) > 0:
        values = steps_of(key, shape, shards, -0.22, 0.18) * values
    return jnp.clip(values, min=-reach, max=reach).astype(held_as)


def setup_inputs(seed: int = 0, part: int = 0) -> dict:
    key_of = jax.random.split(jax.random.key(seed), 4)
    own_keys = jax.random.split(jax.random.fold_in(key_of[3], part), 4)
    return {
        "student": bell_draw(own_keys[0], (ROWS, DS), 1.0, 6.0, ((0, 32), (1, 8))),
        "teacher": bell_draw(own_keys[1], (ROWS, DT), 1.0, 6.0, ((0, 32), (1, 8))),
        "counts": ragged(own_keys[2], SEQS, ROWS, ROWS * 3 // 4, 0).astype(jnp.int32),
    }


def reference(student, teacher, counts):
    seq_ends = jnp.cumsum(counts)
    positions = jnp.arange(ROWS, dtype=jnp.int32)
    segment = lax.optimization_barrier(jnp.sum((positions[:, None] >= seq_ends[None, :-1]).astype(jnp.int32), axis=1))
    same = segment[:, None] == segment[None, :]
    gram_s = jnp.dot(student, student.T, preferred_element_type=jnp.float32) / jnp.sqrt(jnp.float32(DS))
    gram_t = jnp.dot(teacher, teacher.T, preferred_element_type=jnp.float32) / jnp.sqrt(jnp.float32(DT))
    difference = jnp.where(same, gram_s - gram_t, jnp.float32(0.0)).astype(jnp.bfloat16)
    lengths = counts[segment].astype(jnp.float32)
    product = jnp.dot(difference, student, preferred_element_type=jnp.float32)
    return (product / jnp.sqrt(lengths)[:, None]).astype(jnp.bfloat16)
```

```python
import math

import jax
import jax.numpy as jnp
from jax import lax
from jax.sharding import Mesh, PartitionSpec as P

TENSOR = ("y", "xh")
SWAP = [(0, 1), (1, 0)]


def segment_of(positions, seq_ends):
    return jnp.sum((positions[:, None] >= seq_ends[None, :-1]).astype(jnp.int32), axis=1)


def on_device(student, teacher, counts):
    rows, ds = student.shape
    nz, nt = lax.axis_size("z"), lax.axis_size(TENSOR)
    student_scale = 1.0 / math.sqrt(ds * nt)
    teacher_scale = 1.0 / math.sqrt(teacher.shape[1] * nt)
    contraction = (((1,), (1,)), ((), ()))
    z, xl, t = lax.axis_index("z"), lax.axis_index("xl"), lax.axis_index(TENSOR)

    own = jnp.concatenate([student, teacher], axis=1)
    column = lax.all_gather(own, "z", axis=0, tiled=True)
    other = lax.ppermute(own, "xl", SWAP)
    both = jnp.concatenate([own, other], axis=0)
    gram_s = lax.dot_general(
        both[:, :ds], column[:, :ds], contraction, preferred_element_type=jnp.float32
    )
    gram_t = lax.dot_general(
        both[:, ds:], column[:, ds:], contraction, preferred_element_type=jnp.float32
    )
    partial = (gram_s * student_scale - gram_t * teacher_scale).astype(jnp.bfloat16)

    seq_ends = jnp.cumsum(counts)
    r = jnp.arange(rows, dtype=jnp.int32)
    row_of = jnp.concatenate([(2 * z + xl) * rows + r, (2 * z + 1 - xl) * rows + r])
    col_of = ((2 * jnp.arange(nz, dtype=jnp.int32) + xl)[:, None] * rows + r[None, :]).reshape(-1)
    row_segment = segment_of(row_of, seq_ends)
    col_segment = segment_of(col_of, seq_ends)

    share = 2 * rows // nt
    parts = lax.all_to_all(partial.reshape(nt, share, nz * rows), TENSOR, 0, 0)
    summed = jnp.sum(parts.astype(jnp.float32), axis=0)
    my_segment = lax.dynamic_slice(row_segment, (t * share,), (share,))
    difference = jnp.where(my_segment[:, None] == col_segment[None, :], summed, 0.0).astype(
        jnp.bfloat16
    )
    copies = jnp.broadcast_to(difference[None], (nt,) + difference.shape)
    whole = lax.all_to_all(copies, TENSOR, 0, 0).reshape(2 * rows, nz * rows)
    gradient = jnp.dot(whole, column[:, :ds], preferred_element_type=jnp.float32)
    away = lax.ppermute(gradient[rows:].astype(jnp.bfloat16), "xl", SWAP)
    total = gradient[:rows] + away.astype(jnp.float32)

    seq_index = jnp.arange(counts.shape[0], dtype=jnp.int32)
    row_length = jnp.sum(
        jnp.where(row_segment[:rows, None] == seq_index[None, :], counts[None, :], 0), axis=1
    )
    return (total * lax.rsqrt(row_length.astype(jnp.float32))[:, None]).astype(jnp.bfloat16)


def solution(mesh):
    split = Mesh(mesh.devices.reshape(-1, 2, 4, 2, 2), ("z", "xl", "y", "xh", "seq"))
    spec = P(("seq", "z", "xl"), ("y", "xh"))
    return jax.shard_map(
        on_device, mesh=split, in_specs=(spec, spec, P("seq")), out_specs=spec, check_vma=False
    )
```

```python
import math

import jax
import jax.numpy as jnp
from jax import lax
from jax.experimental import pallas as pl
from jax.experimental.pallas import tpu as pltpu
from jax.sharding import Mesh, PartitionSpec as P

TENSOR = ("y", "xh")
ROW = ("z", "xl", "seq")
NZ, NX, NSEQ, NT = 16, 2, 2, 8

ELEMENTS = ((0, 0), (-2, 0), (-4, 1), (3, 0), (3, 1), (4, 0), (4, 1))
FIRST = ((1, 0, (-2, 0)), (3, 0, (3, 0)))
SECOND = ((2, 1, (-2, 1)), (6, 3, (1, 1)), (5, 3, (1, 0)), (4, 3, (0, 1)))
TILES = (
    (0, 0), (0, 1), (0, 3), (0, 4), (0, 5), (0, 6),
    (1, 2), (1, 3), (1, 4), (1, 5), (1, 6),
    (2, 3), (2, 4), (2, 5), (2, 6),
    (3, 4), (3, 5), (3, 6),
)
ONE_SIDED = ((0, 0), (2, 5), (2, 6), (3, 4))
F32, BF16 = jnp.float32, jnp.bfloat16


def place(z, x, s):
    return (z % NZ * NX + x) * NSEQ + s


def moves(step, back):
    pairs = []
    for z in range(NZ):
        for x in range(NX):
            for s in range(NSEQ):
                far = place(z + (step[0] if s == 0 else -step[0]), x ^ step[1], s)
                here = place(z, x, s)
                pairs.append((here, far) if back else (far, here))
    return pairs


def fetch(block, step):
    return lax.ppermute(block, ROW, moves(step, False))


def give(block, step):
    return lax.ppermute(block, ROW, moves(step, True))


def gather(own):
    held = {0: own}
    for group in (FIRST, SECOND):
        for element, source, step in group:
            held[element] = fetch(held[source], step)
    return [held[i] for i in range(len(ELEMENTS))]


def tile_dot(left, right):
    return lax.dot_general(left, right, (((1,), (1,)), ((), ())), preferred_element_type=F32)


def rights_of(left):
    return [b for a, b in TILES if a == left]


def teacher_kernel(scale, *refs):
    blocks, out = refs[:-1], refs[-1]
    k = 0
    for left in sorted({a for a, _ in TILES}):
        rights = rights_of(left)
        right = jnp.concatenate([blocks[b][...] for b in rights], axis=0)
        product = tile_dot(blocks[left][...], right) * scale
        for i in range(len(rights)):
            n = product.shape[0]
            out[k] = product[:, i * n : (i + 1) * n]
            k += 1


def student_kernel(scale, *refs):
    blocks, teacher, out = refs[:-2], refs[-2], refs[-1]
    share = out.shape[1] // len(TILES)
    k = 0
    for left in sorted({a for a, _ in TILES}):
        rights = rights_of(left)
        right = jnp.concatenate([blocks[b][...] for b in rights], axis=0)
        product = tile_dot(blocks[left][...], right) * scale
        for i in range(len(rights)):
            n = product.shape[0]
            tile = (product[:, i * n : (i + 1) * n] - teacher[k]).astype(BF16)
            out[:, k * share : (k + 1) * share, :] = tile.reshape(NT, share, n)
            k += 1


def mask_kernel(where_ref, parts, out):
    share = parts.shape[1] // len(TILES)
    n = parts.shape[2]
    first_end, second_end, part = where_ref[0], where_ref[1], where_ref[2]

    def segment(r):
        return (r >= first_end).astype(jnp.int32) + (r >= second_end).astype(jnp.int32)

    for k, (a, b) in enumerate(TILES):
        rows = slice(k * share, (k + 1) * share)
        total = parts[0, rows, :].astype(F32)
        for s in range(1, NT):
            total += parts[s, rows, :].astype(F32)
        r = where_ref[3 + a] + part * share + lax.broadcasted_iota(jnp.int32, (share, n), 0)
        c = where_ref[3 + b] + lax.broadcasted_iota(jnp.int32, (share, n), 1)
        kept = jnp.where(segment(r) == segment(c), total, 0.0).astype(BF16)
        for s in range(NT):
            out[s, rows, :] = kept


def terms_of(a):
    straight = [(k, b) for k, (p, b) in enumerate(TILES) if p == a]
    turned = [(k, p) for k, (p, b) in enumerate(TILES) if b == a and (p, b) not in ONE_SIDED]
    return straight, turned


def gradient_kernel(wanted, *refs):
    tiles, blocks, outs = refs[0], refs[1 : 1 + len(ELEMENTS)], refs[1 + len(ELEMENTS) :]
    share = tiles.shape[1] // len(TILES)
    n = tiles.shape[2]

    def tile(k):
        return tiles[:, k * share : (k + 1) * share, :].reshape(NT * share, n)

    for out, a in zip(outs, wanted, strict=True):
        straight, turned = terms_of(a)
        total = None
        if straight:
            total = jnp.dot(
                jnp.concatenate([tile(k) for k, _ in straight], axis=1),
                jnp.concatenate([blocks[b][...] for _, b in straight], axis=0),
                preferred_element_type=F32,
            )
        if turned:
            more = lax.dot_general(
                jnp.concatenate([tile(k) for k, _ in turned], axis=0),
                jnp.concatenate([blocks[b][...] for _, b in turned], axis=0),
                (((0,), (0,)), ((), ())),
                preferred_element_type=F32,
            )
            total = more if total is None else total + more
        out[...] = total.astype(out.dtype)


def call(kernel, out_shape, flops, *operands, smem=0):
    vmem = pl.BlockSpec(memory_space=pltpu.VMEM)
    specs = [pl.BlockSpec(memory_space=pltpu.SMEM)] * smem + [vmem] * (len(operands) - smem)
    several = isinstance(out_shape, (list, tuple))
    moved = sum(x.size * x.dtype.itemsize for x in operands)
    return pl.pallas_call(
        kernel,
        out_shape=out_shape,
        in_specs=specs,
        out_specs=[vmem] * len(out_shape) if several else vmem,
        compiler_params=pltpu.CompilerParams(vmem_limit_bytes=40 * 1024 * 1024),
        cost_estimate=pl.CostEstimate(flops=flops, bytes_accessed=moved, transcendentals=0),
    )(*operands)


def on_device(student, teacher, counts):
    rows, ds = student.shape
    dt = teacher.shape[1]
    count = len(TILES)
    share = rows // NT
    z, x, s = lax.axis_index("z"), lax.axis_index("xl"), lax.axis_index("seq")

    teachers = gather(teacher)
    students = gather(student)

    gram_t = call(
        lambda *refs: teacher_kernel(1.0 / math.sqrt(dt * NT), *refs),
        jax.ShapeDtypeStruct((count, rows, rows), F32),
        2 * count * rows * rows * dt,
        *teachers,
    )
    partial = call(
        lambda *refs: student_kernel(1.0 / math.sqrt(ds * NT), *refs),
        jax.ShapeDtypeStruct((NT, count * share, rows), BF16),
        2 * count * rows * rows * ds,
        *students,
        gram_t,
    )

    ends = jnp.cumsum(counts)
    sign = 1 - 2 * s
    starts = [(((z + sign * ez) % NZ) * NX + (x ^ ex)) * rows for ez, ex in ELEMENTS]
    where = jnp.stack([ends[0], ends[1], lax.axis_index(TENSOR)] + starts).astype(jnp.int32)
    parts = lax.all_to_all(partial, TENSOR, 0, 0)
    copies = call(
        mask_kernel,
        jax.ShapeDtypeStruct(parts.shape, BF16),
        NT * count * share * rows,
        where,
        parts,
        smem=1,
    )
    tiles = lax.all_to_all(copies, TENSOR, 0, 0)

    far = [e for e, _, _ in SECOND]
    near = [0] + [e for e, _, _ in FIRST]
    block = 2 * rows * rows * ds
    given = call(
        lambda *refs: gradient_kernel(far, *refs),
        [jax.ShapeDtypeStruct((rows, ds), BF16)] * len(far),
        14 * block,
        tiles,
        *students,
    )
    kept = call(
        lambda *refs: gradient_kernel(near, *refs),
        [jax.ShapeDtypeStruct((rows, ds), F32)] * len(near),
        18 * block,
        tiles,
        *students,
    )
    sums = dict(zip(near, kept, strict=True))
    for (_, target, step), value in zip(SECOND, given, strict=True):
        sums[target] = sums[target] + give(value, step).astype(F32)
    for element, target, step in FIRST:
        sums[target] = sums[target] + give(sums[element].astype(BF16), step).astype(F32)

    r = starts[0] + jnp.arange(rows, dtype=jnp.int32)
    segment = jnp.sum((r[:, None] >= ends[None, :-1]).astype(jnp.int32), axis=1)
    index = jnp.arange(counts.shape[0], dtype=jnp.int32)
    length = jnp.sum(jnp.where(segment[:, None] == index[None, :], counts[None, :], 0), axis=1)
    return (sums[0] * lax.rsqrt(length.astype(F32))[:, None]).astype(BF16)


def solution(mesh):
    split = Mesh(mesh.devices.reshape(NZ, NX, 4, 2, NSEQ), ("z", "xl", "y", "xh", "seq"))
    spec = P(("seq", "z", "xl"), TENSOR)
    return jax.shard_map(
        on_device, mesh=split, in_specs=(spec, spec, P("seq")), out_specs=spec, check_vma=False
    )
```

```python
import math

import jax
import jax.numpy as jnp
from jax import lax
from jax.experimental import pallas as pl
from jax.experimental.pallas import tpu as pltpu
from jax.sharding import Mesh, PartitionSpec as P

TENSOR = ("y", "xh")
ROW = ("z", "xl", "seq")
NZ, NX, NSEQ, NT = 16, 2, 2, 8

ELEMENTS = ((0, 0), (-2, 1), (-4, 1), (3, 0), (3, 1), (4, 0), (4, 1))
FIRST = ((1, 0, (-2, 1)), (3, 0, (3, 0)))
SECOND = ((2, 1, (-2, 0)), (6, 3, (1, 1)), (5, 3, (1, 0)), (4, 3, (0, 1)))
TILES = (
    (0, 0), (0, 1), (0, 3), (0, 4), (0, 5), (0, 6),
    (1, 2), (1, 3), (1, 4), (1, 5), (1, 6),
    (2, 3), (2, 4), (2, 5), (2, 6),
    (3, 4), (3, 5), (3, 6),
)
ONE_SIDED = ((0, 0), (2, 5), (2, 6), (3, 4))
F32, BF16 = jnp.float32, jnp.bfloat16


def place(z, x, s):
    return (z % NZ * NX + x) * NSEQ + s


def moves(step, back):
    pairs = []
    for z in range(NZ):
        for x in range(NX):
            for s in range(NSEQ):
                far = place(z + (step[0] if s == 0 else -step[0]), x ^ step[1], s)
                here = place(z, x, s)
                pairs.append((here, far) if back else (far, here))
    return pairs


def fetch(block, step):
    return lax.ppermute(block, ROW, moves(step, False))


def give(block, step):
    return lax.ppermute(block, ROW, moves(step, True))


def gather(own):
    held = {0: own}
    for group in (FIRST, SECOND):
        for element, source, step in group:
            held[element] = fetch(held[source], step)
    return [held[i] for i in range(len(ELEMENTS))]


def tile_dot(left, right):
    return lax.dot_general(left, right, (((1,), (1,)), ((), ())), preferred_element_type=F32)


def rights_of(left):
    return [b for a, b in TILES if a == left]


def gram_kernel(ds, student_scale, teacher_scale, *refs):
    blocks, out = refs[:-1], refs[-1]
    share = out.shape[1] // len(TILES)
    n = blocks[0].shape[0]
    k = 0
    for left in sorted({a for a, _ in TILES}):
        rights = rights_of(left)
        right_s = jnp.concatenate([blocks[b][:, :ds] for b in rights], axis=0)
        right_t = jnp.concatenate([blocks[b][:, ds:] for b in rights], axis=0)
        product = (
            tile_dot(blocks[left][:, :ds], right_s) * student_scale
            - tile_dot(blocks[left][:, ds:], right_t) * teacher_scale
        )
        for i in range(len(rights)):
            tile = product[:, i * n : (i + 1) * n].astype(BF16)
            out[:, k * share : (k + 1) * share, :] = tile.reshape(NT, share, n)
            k += 1


def mask_kernel(where_ref, parts, out):
    share = parts.shape[1] // len(TILES)
    n = parts.shape[2]
    first_end, second_end, part = where_ref[0], where_ref[1], where_ref[2]

    def segment(r):
        return (r >= first_end).astype(jnp.int32) + (r >= second_end).astype(jnp.int32)

    for k, (a, b) in enumerate(TILES):
        rows = slice(k * share, (k + 1) * share)
        total = parts[0, rows, :].astype(F32)
        for s in range(1, NT):
            total += parts[s, rows, :].astype(F32)
        r = where_ref[3 + a] + part * share + lax.broadcasted_iota(jnp.int32, (share, n), 0)
        c = where_ref[3 + b] + lax.broadcasted_iota(jnp.int32, (share, n), 1)
        kept = jnp.where(segment(r) == segment(c), total, 0.0).astype(BF16)
        for s in range(NT):
            out[s, rows, :] = kept


def terms_of(a):
    straight = [(k, b) for k, (p, b) in enumerate(TILES) if p == a]
    turned = [(k, p) for k, (p, b) in enumerate(TILES) if b == a and (p, b) not in ONE_SIDED]
    return straight, turned


def gradient_kernel(wanted, *refs):
    tiles, blocks, outs = refs[0], refs[1 : 1 + len(ELEMENTS)], refs[1 + len(ELEMENTS) :]
    share = tiles.shape[1] // len(TILES)
    n, width = tiles.shape[2], outs[0].shape[1]

    def tile(k):
        return tiles[:, k * share : (k + 1) * share, :].reshape(NT * share, n)

    for out, a in zip(outs, wanted, strict=True):
        straight, turned = terms_of(a)
        total = None
        if straight:
            total = jnp.dot(
                jnp.concatenate([tile(k) for k, _ in straight], axis=1),
                jnp.concatenate([blocks[b][:, :width] for _, b in straight], axis=0),
                preferred_element_type=F32,
            )
        if turned:
            more = lax.dot_general(
                jnp.concatenate([tile(k) for k, _ in turned], axis=0),
                jnp.concatenate([blocks[b][:, :width] for _, b in turned], axis=0),
                (((0,), (0,)), ((), ())),
                preferred_element_type=F32,
            )
            total = more if total is None else total + more
        out[...] = total.astype(out.dtype)


def call(kernel, out_shape, flops, *operands, smem=0):
    vmem = pl.BlockSpec(memory_space=pltpu.VMEM)
    specs = [pl.BlockSpec(memory_space=pltpu.SMEM)] * smem + [vmem] * (len(operands) - smem)
    several = isinstance(out_shape, (list, tuple))
    moved = sum(x.size * x.dtype.itemsize for x in operands)
    return pl.pallas_call(
        kernel,
        out_shape=out_shape,
        in_specs=specs,
        out_specs=[vmem] * len(out_shape) if several else vmem,
        compiler_params=pltpu.CompilerParams(vmem_limit_bytes=40 * 1024 * 1024),
        cost_estimate=pl.CostEstimate(flops=flops, bytes_accessed=moved, transcendentals=0),
    )(*operands)


def on_device(student, teacher, counts):
    rows, ds = student.shape
    dt = teacher.shape[1]
    count = len(TILES)
    share = rows // NT
    z, x, s = lax.axis_index("z"), lax.axis_index("xl"), lax.axis_index("seq")

    blocks = gather(jnp.concatenate([student, teacher], axis=1))
    partial = call(
        lambda *refs: gram_kernel(
            ds, 1.0 / math.sqrt(ds * NT), 1.0 / math.sqrt(dt * NT), *refs
        ),
        jax.ShapeDtypeStruct((NT, count * share, rows), BF16),
        2 * count * rows * rows * (ds + dt),
        *blocks,
    )

    ends = jnp.cumsum(counts)
    sign = 1 - 2 * s
    starts = [(((z + sign * ez) % NZ) * NX + (x ^ ex)) * rows for ez, ex in ELEMENTS]
    where = jnp.stack([ends[0], ends[1], lax.axis_index(TENSOR)] + starts).astype(jnp.int32)
    parts = lax.all_to_all(partial, TENSOR, 0, 0)
    copies = call(
        mask_kernel,
        jax.ShapeDtypeStruct(parts.shape, BF16),
        NT * count * share * rows,
        where,
        parts,
        smem=1,
    )
    tiles = lax.all_to_all(copies, TENSOR, 0, 0)

    far = [e for e, _, _ in SECOND]
    near = [0] + [e for e, _, _ in FIRST]
    block = 2 * rows * rows * ds
    given = call(
        lambda *refs: gradient_kernel(far, *refs),
        [jax.ShapeDtypeStruct((rows, ds), BF16)] * len(far),
        14 * block,
        tiles,
        *blocks,
    )
    kept = call(
        lambda *refs: gradient_kernel(near, *refs),
        [jax.ShapeDtypeStruct((rows, ds), F32)] * len(near),
        18 * block,
        tiles,
        *blocks,
    )
    sums = dict(zip(near, kept, strict=True))
    for (_, target, step), value in zip(SECOND, given, strict=True):
        sums[target] = sums[target] + give(value, step).astype(F32)
    for element, target, step in FIRST:
        sums[target] = sums[target] + give(sums[element].astype(BF16), step).astype(F32)

    r = starts[0] + jnp.arange(rows, dtype=jnp.int32)
    segment = jnp.sum((r[:, None] >= ends[None, :-1]).astype(jnp.int32), axis=1)
    index = jnp.arange(counts.shape[0], dtype=jnp.int32)
    length = jnp.sum(jnp.where(segment[:, None] == index[None, :], counts[None, :], 0), axis=1)
    return (sums[0] * lax.rsqrt(length.astype(F32))[:, None]).astype(BF16)


def solution(mesh):
    split = Mesh(mesh.devices.reshape(NZ, NX, 4, 2, NSEQ), ("z", "xl", "y", "xh", "seq"))
    spec = P(("seq", "z", "xl"), TENSOR)
    return jax.shard_map(
        on_device, mesh=split, in_specs=(spec, spec, P("seq")), out_specs=spec, check_vma=False
    )
```

```python
import math

import jax
import jax.numpy as jnp
from jax import lax
from jax.experimental import pallas as pl
from jax.experimental.pallas import tpu as pltpu
from jax.sharding import Mesh, PartitionSpec as P

TENSOR = ("y", "xh")
ROW = ("z", "xl", "seq")
NZ, NX, NSEQ, NT = 16, 2, 2, 8

ELEMENTS = ((0, 0), (1, 0), (0, 1), (-3, 0), (1, 1), (2, 0), (2, 1), (-6, 0))
FIRST = ((3, 0, (-3, 0)), (1, 0, (1, 0)), (2, 0, (0, 1)))
SECOND = ((7, 3, (-3, 0)), (5, 1, (1, 0)), (6, 1, (1, 1)), (4, 1, (0, 1)))
TILES = (
    (0, 0), (0, 1), (0, 2), (0, 3), (0, 5), (0, 6),
    (1, 2),
    (3, 1), (3, 2), (3, 4), (3, 5), (3, 6),
    (7, 0), (7, 1), (7, 2), (7, 4), (7, 5), (7, 6),
)
ONE_SIDED = ((0, 0), (0, 2), (7, 5), (7, 6))
F32, BF16 = jnp.float32, jnp.bfloat16


def place(z, x, s):
    return (z % NZ * NX + x) * NSEQ + s


def moves(step, back):
    pairs = []
    for z in range(NZ):
        for x in range(NX):
            for s in range(NSEQ):
                far = place(z + (step[0] if s == 0 else -step[0]), x ^ step[1], s)
                here = place(z, x, s)
                pairs.append((here, far) if back else (far, here))
    return pairs


def fetch(block, step):
    return lax.ppermute(block, ROW, moves(step, False))


def give(block, step):
    return lax.ppermute(block, ROW, moves(step, True))


def gather(own):
    held = {0: own}
    for group in (FIRST, SECOND):
        for element, source, step in group:
            held[element] = fetch(held[source], step)
    return [held[i] for i in range(len(ELEMENTS))]


def tile_dot(left, right):
    return lax.dot_general(left, right, (((1,), (1,)), ((), ())), preferred_element_type=F32)


def rights_of(left):
    return [b for a, b in TILES if a == left]


def gram_kernel(ds, student_scale, teacher_scale, *refs):
    blocks, out = refs[:-1], refs[-1]
    share = out.shape[1] // len(TILES)
    n = blocks[0].shape[0]
    k = 0
    for left in sorted({a for a, _ in TILES}):
        rights = rights_of(left)
        right_s = jnp.concatenate([blocks[b][:, :ds] for b in rights], axis=0)
        right_t = jnp.concatenate([blocks[b][:, ds:] for b in rights], axis=0)
        product = (
            tile_dot(blocks[left][:, :ds], right_s) * student_scale
            - tile_dot(blocks[left][:, ds:], right_t) * teacher_scale
        )
        for i in range(len(rights)):
            tile = product[:, i * n : (i + 1) * n].astype(BF16)
            out[:, k * share : (k + 1) * share, :] = tile.reshape(NT, share, n)
            k += 1


def mask_kernel(where_ref, parts, out):
    share = parts.shape[1] // len(TILES)
    n = parts.shape[2]
    first_end, second_end, part = where_ref[0], where_ref[1], where_ref[2]

    def segment(r):
        return (r >= first_end).astype(jnp.int32) + (r >= second_end).astype(jnp.int32)

    for k, (a, b) in enumerate(TILES):
        rows = slice(k * share, (k + 1) * share)
        total = parts[0, rows, :].astype(F32)
        for s in range(1, NT):
            total += parts[s, rows, :].astype(F32)
        r = where_ref[3 + a] + part * share + lax.broadcasted_iota(jnp.int32, (share, n), 0)
        c = where_ref[3 + b] + lax.broadcasted_iota(jnp.int32, (share, n), 1)
        kept = jnp.where(segment(r) == segment(c), total, 0.0).astype(BF16)
        for s in range(NT):
            out[s, rows, :] = kept


def terms_of(a):
    straight = [(k, b) for k, (p, b) in enumerate(TILES) if p == a]
    turned = [(k, p) for k, (p, b) in enumerate(TILES) if b == a and (p, b) not in ONE_SIDED]
    return straight, turned


def gradient_kernel(wanted, *refs):
    tiles, blocks, outs = refs[0], refs[1 : 1 + len(ELEMENTS)], refs[1 + len(ELEMENTS) :]
    share = tiles.shape[1] // len(TILES)
    n, width = tiles.shape[2], outs[0].shape[1]

    def tile(k):
        return tiles[:, k * share : (k + 1) * share, :].reshape(NT * share, n)

    for out, a in zip(outs, wanted, strict=True):
        straight, turned = terms_of(a)
        total = None
        if straight:
            total = jnp.dot(
                jnp.concatenate([tile(k) for k, _ in straight], axis=1),
                jnp.concatenate([blocks[b][:, :width] for _, b in straight], axis=0),
                preferred_element_type=F32,
            )
        if turned:
            more = lax.dot_general(
                jnp.concatenate([tile(k) for k, _ in turned], axis=0),
                jnp.concatenate([blocks[b][:, :width] for _, b in turned], axis=0),
                (((0,), (0,)), ((), ())),
                preferred_element_type=F32,
            )
            total = more if total is None else total + more
        out[...] = total.astype(out.dtype)


def call(kernel, out_shape, flops, *operands, smem=0):
    vmem = pl.BlockSpec(memory_space=pltpu.VMEM)
    specs = [pl.BlockSpec(memory_space=pltpu.SMEM)] * smem + [vmem] * (len(operands) - smem)
    several = isinstance(out_shape, (list, tuple))
    moved = sum(x.size * x.dtype.itemsize for x in operands)
    return pl.pallas_call(
        kernel,
        out_shape=out_shape,
        in_specs=specs,
        out_specs=[vmem] * len(out_shape) if several else vmem,
        compiler_params=pltpu.CompilerParams(vmem_limit_bytes=40 * 1024 * 1024),
        cost_estimate=pl.CostEstimate(flops=flops, bytes_accessed=moved, transcendentals=0),
    )(*operands)


def on_device(student, teacher, counts):
    rows, ds = student.shape
    dt = teacher.shape[1]
    count = len(TILES)
    share = rows // NT
    z, x, s = lax.axis_index("z"), lax.axis_index("xl"), lax.axis_index("seq")

    blocks = gather(jnp.concatenate([student, teacher], axis=1))
    partial = call(
        lambda *refs: gram_kernel(
            ds, 1.0 / math.sqrt(ds * NT), 1.0 / math.sqrt(dt * NT), *refs
        ),
        jax.ShapeDtypeStruct((NT, count * share, rows), BF16),
        2 * count * rows * rows * (ds + dt),
        *blocks,
    )

    ends = jnp.cumsum(counts)
    sign = 1 - 2 * s
    starts = [(((z + sign * ez) % NZ) * NX + (x ^ ex)) * rows for ez, ex in ELEMENTS]
    where = jnp.stack([ends[0], ends[1], lax.axis_index(TENSOR)] + starts).astype(jnp.int32)
    parts = lax.all_to_all(partial, TENSOR, 0, 0)
    copies = call(
        mask_kernel,
        jax.ShapeDtypeStruct(parts.shape, BF16),
        NT * count * share * rows,
        where,
        parts,
        smem=1,
    )
    tiles = lax.all_to_all(copies, TENSOR, 0, 0)

    far = [7, 3, 6, 5, 4, 1, 2]
    block = 2 * rows * rows * ds
    given = call(
        lambda *refs: gradient_kernel(far, *refs),
        [jax.ShapeDtypeStruct((rows, ds), BF16)] * len(far),
        26 * block,
        tiles,
        *blocks,
    )
    total = call(
        lambda *refs: gradient_kernel([0], *refs),
        jax.ShapeDtypeStruct((rows, ds), F32),
        6 * block,
        tiles,
        *blocks,
    )
    for e, value in zip(far, given, strict=True):
        total = total + give(value, ELEMENTS[e]).astype(F32)

    r = starts[0] + jnp.arange(rows, dtype=jnp.int32)
    segment = jnp.sum((r[:, None] >= ends[None, :-1]).astype(jnp.int32), axis=1)
    index = jnp.arange(counts.shape[0], dtype=jnp.int32)
    length = jnp.sum(jnp.where(segment[:, None] == index[None, :], counts[None, :], 0), axis=1)
    return (total * lax.rsqrt(length.astype(F32))[:, None]).astype(BF16)


def solution(mesh):
    split = Mesh(mesh.devices.reshape(NZ, NX, 4, 2, NSEQ), ("z", "xl", "y", "xh", "seq"))
    spec = P(("seq", "z", "xl"), TENSOR)
    return jax.shard_map(
        on_device, mesh=split, in_specs=(spec, spec, P("seq")), out_specs=spec, check_vma=False
    )
```

```python
import math

import jax
import jax.numpy as jnp
from jax import lax
from jax.experimental import pallas as pl
from jax.experimental.pallas import tpu as pltpu
from jax.sharding import Mesh, PartitionSpec as P

TENSOR = ("y", "xh")
ROW = ("z", "xl", "seq")
NZ, NX, NSEQ, NT = 16, 2, 2, 8

ELEMENTS = ((0, 0), (-2, 1), (-4, 1), (3, 0), (3, 1), (4, 0), (4, 1))
FIRST = ((1, 0, (-2, 1)), (3, 0, (3, 0)))
SECOND = ((2, 1, (-2, 0)), (6, 3, (1, 1)), (5, 3, (1, 0)), (4, 3, (0, 1)))
TILES = (
    (0, 0), (0, 1), (0, 3), (0, 4), (0, 5), (0, 6),
    (1, 2), (1, 3), (1, 4), (1, 5), (1, 6),
    (2, 3), (2, 4), (2, 5), (2, 6),
    (3, 4), (3, 5), (3, 6),
)
ONE_SIDED = ((0, 0), (2, 5), (2, 6), (3, 4))
F32, BF16 = jnp.float32, jnp.bfloat16


def place(z, x, s):
    return (z % NZ * NX + x) * NSEQ + s


def moves(step, back):
    pairs = []
    for z in range(NZ):
        for x in range(NX):
            for s in range(NSEQ):
                far = place(z + (step[0] if s == 0 else -step[0]), x ^ step[1], s)
                here = place(z, x, s)
                pairs.append((here, far) if back else (far, here))
    return pairs


def fetch(block, step):
    return lax.ppermute(block, ROW, moves(step, False))


def give(block, step):
    return lax.ppermute(block, ROW, moves(step, True))


def gather(own):
    held = {0: own}
    for group in (FIRST, SECOND):
        for element, source, step in group:
            held[element] = fetch(held[source], step)
    return [held[i] for i in range(len(ELEMENTS))]


def tile_dot(left, right):
    return lax.dot_general(left, right, (((1,), (1,)), ((), ())), preferred_element_type=F32)


def rights_of(left):
    return [b for a, b in TILES if a == left]


def gram_kernel(ds, student_scale, teacher_scale, *refs):
    blocks, out = refs[:-1], refs[-1]
    share = out.shape[1] // len(TILES)
    n = blocks[0].shape[0]
    k = 0
    for left in sorted({a for a, _ in TILES}):
        rights = rights_of(left)
        right_s = jnp.concatenate([blocks[b][:, :ds] for b in rights], axis=0)
        right_t = jnp.concatenate([blocks[b][:, ds:] for b in rights], axis=0)
        product = (
            tile_dot(blocks[left][:, :ds], right_s) * student_scale
            - tile_dot(blocks[left][:, ds:], right_t) * teacher_scale
        )
        for i in range(len(rights)):
            tile = product[:, i * n : (i + 1) * n].astype(BF16)
            out[:, k * share : (k + 1) * share, :] = tile.reshape(NT, share, n)
            k += 1


def mask_kernel(where_ref, parts, out):
    share = parts.shape[1] // len(TILES)
    n = parts.shape[2]
    first_end, second_end, part = where_ref[0], where_ref[1], where_ref[2]

    def segment(r):
        return (r >= first_end).astype(jnp.int32) + (r >= second_end).astype(jnp.int32)

    for k, (a, b) in enumerate(TILES):
        rows = slice(k * share, (k + 1) * share)
        total = parts[0, rows, :].astype(F32)
        for s in range(1, NT):
            total += parts[s, rows, :].astype(F32)
        r = where_ref[3 + a] + part * share + lax.broadcasted_iota(jnp.int32, (share, n), 0)
        c = where_ref[3 + b] + lax.broadcasted_iota(jnp.int32, (share, n), 1)
        kept = jnp.where(segment(r) == segment(c), total, 0.0).astype(BF16)
        for s in range(NT):
            out[s, rows, :] = kept


def terms_of(a):
    straight = [(k, b) for k, (p, b) in enumerate(TILES) if p == a]
    turned = [(k, p) for k, (p, b) in enumerate(TILES) if b == a and (p, b) not in ONE_SIDED]
    return straight, turned


def gradient_kernel(wanted, *refs):
    tiles, blocks, outs = refs[0], refs[1 : 1 + len(ELEMENTS)], refs[1 + len(ELEMENTS) :]
    share = tiles.shape[1] // len(TILES)
    n, width = tiles.shape[2], outs[0].shape[1]

    def tile(k):
        return tiles[:, k * share : (k + 1) * share, :].reshape(NT * share, n)

    for out, a in zip(outs, wanted, strict=True):
        straight, turned = terms_of(a)
        total = None
        if straight:
            total = jnp.dot(
                jnp.concatenate([tile(k) for k, _ in straight], axis=1),
                jnp.concatenate([blocks[b][:, :width] for _, b in straight], axis=0),
                preferred_element_type=F32,
            )
        if turned:
            more = lax.dot_general(
                jnp.concatenate([tile(k) for k, _ in turned], axis=0),
                jnp.concatenate([blocks[b][:, :width] for _, b in turned], axis=0),
                (((0,), (0,)), ((), ())),
                preferred_element_type=F32,
            )
            total = more if total is None else total + more
        out[...] = total.astype(out.dtype)


def call(kernel, out_shape, flops, *operands, smem=0):
    vmem = pl.BlockSpec(memory_space=pltpu.VMEM)
    specs = [pl.BlockSpec(memory_space=pltpu.SMEM)] * smem + [vmem] * (len(operands) - smem)
    several = isinstance(out_shape, (list, tuple))
    moved = sum(x.size * x.dtype.itemsize for x in operands)
    return pl.pallas_call(
        kernel,
        out_shape=out_shape,
        in_specs=specs,
        out_specs=[vmem] * len(out_shape) if several else vmem,
        compiler_params=pltpu.CompilerParams(vmem_limit_bytes=16 * 1024 * 1024),
        cost_estimate=pl.CostEstimate(flops=flops, bytes_accessed=moved, transcendentals=0),
    )(*operands)


def on_device(student, teacher, counts):
    rows, ds = student.shape
    dt = teacher.shape[1]
    count = len(TILES)
    share = rows // NT
    z, x, s = lax.axis_index("z"), lax.axis_index("xl"), lax.axis_index("seq")

    blocks = gather(jnp.concatenate([student, teacher], axis=1))
    partial = call(
        lambda *refs: gram_kernel(
            ds, 1.0 / math.sqrt(ds * NT), 1.0 / math.sqrt(dt * NT), *refs
        ),
        jax.ShapeDtypeStruct((NT, count * share, rows), BF16),
        2 * count * rows * rows * (ds + dt),
        *blocks,
    )

    ends = jnp.cumsum(counts)
    sign = 1 - 2 * s
    starts = [(((z + sign * ez) % NZ) * NX + (x ^ ex)) * rows for ez, ex in ELEMENTS]
    where = jnp.stack([ends[0], ends[1], lax.axis_index(TENSOR)] + starts).astype(jnp.int32)
    parts = lax.all_to_all(partial, TENSOR, 0, 0)
    copies = call(
        mask_kernel,
        jax.ShapeDtypeStruct(parts.shape, BF16),
        NT * count * share * rows,
        where,
        parts,
        smem=1,
    )
    tiles = lax.all_to_all(copies, TENSOR, 0, 0)

    far = [e for e, _, _ in SECOND]
    near = [0] + [e for e, _, _ in FIRST]
    block = 2 * rows * rows * ds
    given = call(
        lambda *refs: gradient_kernel(far, *refs),
        [jax.ShapeDtypeStruct((rows, ds), BF16)] * len(far),
        14 * block,
        tiles,
        student,
        *blocks[1:],
    )
    kept = call(
        lambda *refs: gradient_kernel(near, *refs),
        [jax.ShapeDtypeStruct((rows, ds), F32)] * len(near),
        18 * block,
        tiles,
        student,
        *blocks[1:],
    )
    sums = dict(zip(near, kept, strict=True))
    for (_, target, step), value in zip(SECOND, given, strict=True):
        sums[target] = sums[target] + give(value, step).astype(F32)
    for element, target, step in FIRST:
        sums[target] = sums[target] + give(sums[element].astype(BF16), step).astype(F32)

    r = starts[0] + jnp.arange(rows, dtype=jnp.int32)
    segment = jnp.sum((r[:, None] >= ends[None, :-1]).astype(jnp.int32), axis=1)
    index = jnp.arange(counts.shape[0], dtype=jnp.int32)
    length = jnp.sum(jnp.where(segment[:, None] == index[None, :], counts[None, :], 0), axis=1)
    return (sums[0] * lax.rsqrt(length.astype(F32))[:, None]).astype(BF16)


def solution(mesh):
    split = Mesh(mesh.devices.reshape(NZ, NX, 4, 2, NSEQ), ("z", "xl", "y", "xh", "seq"))
    spec = P(("seq", "z", "xl"), TENSOR)
    return jax.shard_map(
        on_device, mesh=split, in_specs=(spec, spec, P("seq")), out_specs=spec, check_vma=False
    )
```

```python
import math

import jax
import jax.numpy as jnp
from jax import lax
from jax.experimental import pallas as pl
from jax.experimental.pallas import tpu as pltpu
from jax.sharding import Mesh, PartitionSpec as P

TENSOR = ("y", "xh")
ROW = ("z", "xl", "seq")
NZ, NX, NSEQ, NT = 16, 2, 2, 8

ELEMENTS = ((0, 0), (-2, 1), (-4, 1), (3, 0), (3, 1), (4, 0), (4, 1))
FIRST = ((1, 0, (-2, 1)), (3, 0, (3, 0)))
SECOND = ((2, 1, (-2, 0)), (6, 3, (1, 1)), (5, 3, (1, 0)), (4, 3, (0, 1)))
TILES = (
    (0, 0), (0, 1), (0, 3), (0, 4), (0, 5), (0, 6),
    (1, 2), (1, 3), (1, 4), (1, 5), (1, 6),
    (2, 3), (2, 4), (2, 5), (2, 6),
    (3, 4), (3, 5), (3, 6),
)
ONE_SIDED = ((0, 0), (2, 5), (2, 6), (3, 4))
F32, BF16 = jnp.float32, jnp.bfloat16


def place(z, x, s):
    return (z % NZ * NX + x) * NSEQ + s


def moves(step, back):
    pairs = []
    for z in range(NZ):
        for x in range(NX):
            for s in range(NSEQ):
                far = place(z + (step[0] if s == 0 else -step[0]), x ^ step[1], s)
                here = place(z, x, s)
                pairs.append((here, far) if back else (far, here))
    return pairs


def fetch(block, step):
    return lax.ppermute(block, ROW, moves(step, False))


def give(block, step):
    return lax.ppermute(block, ROW, moves(step, True))


def gather(own):
    held = {0: own}
    for group in (FIRST, SECOND):
        for element, source, step in group:
            held[element] = fetch(held[source], step)
    return [held[i] for i in range(len(ELEMENTS))]


def tile_dot(left, right):
    return lax.dot_general(left, right, (((1,), (1,)), ((), ())), preferred_element_type=F32)


def rights_of(left):
    return [b for a, b in TILES if a == left]


def gram_kernel(ds, student_scale, teacher_scale, *refs):
    blocks, out = refs[:-1], refs[-1]
    share = out.shape[1] // len(TILES)
    n = blocks[0].shape[0]
    k = 0
    for left in sorted({a for a, _ in TILES}):
        rights = rights_of(left)
        right_s = jnp.concatenate([blocks[b][:, :ds] for b in rights], axis=0)
        right_t = jnp.concatenate([blocks[b][:, ds:] for b in rights], axis=0)
        product = (
            tile_dot(blocks[left][:, :ds], right_s) * student_scale
            - tile_dot(blocks[left][:, ds:], right_t) * teacher_scale
        )
        for i in range(len(rights)):
            tile = product[:, i * n : (i + 1) * n].astype(BF16)
            out[:, k * share : (k + 1) * share, :] = tile.reshape(NT, share, n)
            k += 1


def mask_kernel(where_ref, parts, out):
    share = parts.shape[1] // len(TILES)
    n = parts.shape[2]
    first_end, second_end, part = where_ref[0], where_ref[1], where_ref[2]

    def segment(r):
        return (r >= first_end).astype(jnp.int32) + (r >= second_end).astype(jnp.int32)

    for k, (a, b) in enumerate(TILES):
        rows = slice(k * share, (k + 1) * share)
        total = parts[0, rows, :].astype(F32)
        for s in range(1, NT):
            total += parts[s, rows, :].astype(F32)
        r = where_ref[3 + a] + part * share + lax.broadcasted_iota(jnp.int32, (share, n), 0)
        c = where_ref[3 + b] + lax.broadcasted_iota(jnp.int32, (share, n), 1)
        kept = jnp.where(segment(r) == segment(c), total, 0.0).astype(BF16)
        for s in range(NT):
            out[s, rows, :] = kept


def terms_of(a):
    straight = [(k, b) for k, (p, b) in enumerate(TILES) if p == a]
    turned = [(k, p) for k, (p, b) in enumerate(TILES) if b == a and (p, b) not in ONE_SIDED]
    return straight, turned


def gradient_kernel(wanted, *refs):
    tiles, blocks, outs = refs[0], refs[1 : 1 + len(ELEMENTS)], refs[1 + len(ELEMENTS) :]
    share = tiles.shape[1] // len(TILES)
    n, width = tiles.shape[2], outs[0].shape[1]

    def tile(k):
        return tiles[:, k * share : (k + 1) * share, :].reshape(NT * share, n)

    for out, a in zip(outs, wanted, strict=True):
        straight, turned = terms_of(a)
        total = None
        if straight:
            total = jnp.dot(
                jnp.concatenate([tile(k) for k, _ in straight], axis=1),
                jnp.concatenate([blocks[b][:, :width] for _, b in straight], axis=0),
                preferred_element_type=F32,
            )
        if turned:
            more = lax.dot_general(
                jnp.concatenate([tile(k) for k, _ in turned], axis=0),
                jnp.concatenate([blocks[b][:, :width] for _, b in turned], axis=0),
                (((0,), (0,)), ((), ())),
                preferred_element_type=F32,
            )
            total = more if total is None else total + more
        out[...] = total.astype(out.dtype)


def call(kernel, out_shape, flops, *operands, smem=0):
    vmem = pl.BlockSpec(memory_space=pltpu.VMEM)
    specs = [pl.BlockSpec(memory_space=pltpu.SMEM)] * smem + [vmem] * (len(operands) - smem)
    several = isinstance(out_shape, (list, tuple))
    moved = sum(x.size * x.dtype.itemsize for x in operands)
    return pl.pallas_call(
        kernel,
        out_shape=out_shape,
        in_specs=specs,
        out_specs=[vmem] * len(out_shape) if several else vmem,
        compiler_params=pltpu.CompilerParams(vmem_limit_bytes=16 * 1024 * 1024),
        cost_estimate=pl.CostEstimate(flops=flops, bytes_accessed=moved, transcendentals=0),
    )(*operands)


def on_device(student, teacher, counts):
    rows, ds = student.shape
    dt = teacher.shape[1]
    count = len(TILES)
    share = rows // NT
    z, x, s = lax.axis_index("z"), lax.axis_index("xl"), lax.axis_index("seq")

    blocks = gather(jnp.concatenate([student, teacher], axis=1))
    ends = jnp.cumsum(counts)
    sign = 1 - 2 * s
    starts = [(((z + sign * ez) % NZ) * NX + (x ^ ex)) * rows for ez, ex in ELEMENTS]
    where = jnp.stack([ends[0], ends[1], lax.axis_index(TENSOR)] + starts).astype(jnp.int32)
    r = starts[0] + jnp.arange(rows, dtype=jnp.int32)
    segment = jnp.sum((r[:, None] >= ends[None, :-1]).astype(jnp.int32), axis=1)
    index = jnp.arange(counts.shape[0], dtype=jnp.int32)
    length = jnp.sum(jnp.where(segment[:, None] == index[None, :], counts[None, :], 0), axis=1)
    scale = lax.rsqrt(length.astype(F32))
    where, scale, *blocks = lax.optimization_barrier((where, scale, *blocks))
    partial = call(
        lambda *refs: gram_kernel(
            ds, 1.0 / math.sqrt(ds * NT), 1.0 / math.sqrt(dt * NT), *refs
        ),
        jax.ShapeDtypeStruct((NT, count * share, rows), BF16),
        2 * count * rows * rows * (ds + dt),
        *blocks,
    )

    parts = lax.all_to_all(partial, TENSOR, 0, 0)
    copies = call(
        mask_kernel,
        jax.ShapeDtypeStruct(parts.shape, BF16),
        NT * count * share * rows,
        where,
        parts,
        smem=1,
    )
    tiles = lax.all_to_all(copies, TENSOR, 0, 0)

    far = [e for e, _, _ in SECOND]
    near = [0] + [e for e, _, _ in FIRST]
    block = 2 * rows * rows * ds
    given = call(
        lambda *refs: gradient_kernel(far, *refs),
        [jax.ShapeDtypeStruct((rows, ds), BF16)] * len(far),
        14 * block,
        tiles,
        student,
        *blocks[1:],
    )
    kept = call(
        lambda *refs: gradient_kernel(near, *refs),
        [jax.ShapeDtypeStruct((rows, ds), F32)] * len(near),
        18 * block,
        tiles,
        student,
        *blocks[1:],
    )
    sums = dict(zip(near, kept, strict=True))
    for (_, target, step), value in zip(SECOND, given, strict=True):
        sums[target] = sums[target] + give(value, step).astype(F32)
    for element, target, step in FIRST:
        sums[target] = sums[target] + give(sums[element].astype(BF16), step).astype(F32)

    return (sums[0] * scale[:, None]).astype(BF16)


def solution(mesh):
    split = Mesh(mesh.devices.reshape(NZ, NX, 4, 2, NSEQ), ("z", "xl", "y", "xh", "seq"))
    spec = P(("seq", "z", "xl"), TENSOR)
    return jax.shard_map(
        on_device, mesh=split, in_specs=(spec, spec, P("seq")), out_specs=spec, check_vma=False
    )
```

```python
import math

import jax
import jax.numpy as jnp
from jax import lax
from jax.experimental import pallas as pl
from jax.experimental.pallas import tpu as pltpu
from jax.sharding import Mesh, PartitionSpec as P

TENSOR = ("y", "xh")
ROW = ("z", "xl", "seq")
NZ, NX, NSEQ, NT = 16, 2, 2, 8

ELEMENTS = ((0, 0), (-2, 1), (-4, 1), (3, 0), (3, 1), (4, 0), (4, 1))
FIRST = ((1, 0, (-2, 1)), (3, 0, (3, 0)))
SECOND = ((2, 1, (-2, 0)), (6, 3, (1, 1)), (5, 3, (1, 0)), (4, 3, (0, 1)))
TILES = (
    (0, 0), (0, 1), (0, 3), (0, 4), (0, 5), (0, 6),
    (1, 2), (1, 3), (1, 4), (1, 5), (1, 6),
    (2, 3), (2, 4), (2, 5), (2, 6),
    (3, 4), (3, 5), (3, 6),
)
BATCHES = (((0, 1, 2), (3, 4, 5, 6)), ((3,), (4, 5, 6)), ((0,), (0, 1)), ((1,), (2,)))
ONE_SIDED = ((0, 0), (2, 5), (2, 6), (3, 4))
F32, BF16 = jnp.float32, jnp.bfloat16


def place(z, x, s):
    return (z % NZ * NX + x) * NSEQ + s


def moves(step, back):
    pairs = []
    for z in range(NZ):
        for x in range(NX):
            for s in range(NSEQ):
                far = place(z + (step[0] if s == 0 else -step[0]), x ^ step[1], s)
                here = place(z, x, s)
                pairs.append((here, far) if back else (far, here))
    return pairs


def fetch(block, step):
    return lax.ppermute(block, ROW, moves(step, False))


def give(block, step):
    return lax.ppermute(block, ROW, moves(step, True))


def gather(own):
    held = {0: own}
    for group in (FIRST, SECOND):
        for element, source, step in group:
            held[element] = fetch(held[source], step)
    return [held[i] for i in range(len(ELEMENTS))]


def tile_dot(left, right):
    return lax.dot_general(left, right, (((1,), (1,)), ((), ())), preferred_element_type=F32)


def gram_kernel(ds, student_scale, teacher_scale, *refs):
    blocks, out = refs[:-1], refs[-1]
    share = out.shape[1] // len(TILES)
    n = blocks[0].shape[0]

    def rows_of(elements, columns):
        return jnp.concatenate([blocks[e][:, columns] for e in elements], axis=0)

    for lefts, rights in BATCHES:
        product = (
            tile_dot(rows_of(lefts, slice(0, ds)), rows_of(rights, slice(0, ds))) * student_scale
            - tile_dot(rows_of(lefts, slice(ds, None)), rows_of(rights, slice(ds, None)))
            * teacher_scale
        )
        for i, a in enumerate(lefts):
            for j, b in enumerate(rights):
                k = TILES.index((a, b))
                tile = product[i * n : (i + 1) * n, j * n : (j + 1) * n].astype(BF16)
                out[:, k * share : (k + 1) * share, :] = tile.reshape(NT, share, n)


def mask_kernel(where_ref, parts, out):
    share = parts.shape[1] // len(TILES)
    n = parts.shape[2]
    first_end, second_end, part = where_ref[0], where_ref[1], where_ref[2]

    def segment(r):
        return (r >= first_end).astype(jnp.int32) + (r >= second_end).astype(jnp.int32)

    for k, (a, b) in enumerate(TILES):
        rows = slice(k * share, (k + 1) * share)
        total = parts[0, rows, :].astype(F32)
        for s in range(1, NT):
            total += parts[s, rows, :].astype(F32)
        r = where_ref[3 + a] + part * share + lax.broadcasted_iota(jnp.int32, (share, n), 0)
        c = where_ref[3 + b] + lax.broadcasted_iota(jnp.int32, (share, n), 1)
        kept = jnp.where(segment(r) == segment(c), total, 0.0).astype(BF16)
        for s in range(NT):
            out[s, rows, :] = kept


def terms_of(a):
    straight = [(k, b) for k, (p, b) in enumerate(TILES) if p == a]
    turned = [(k, p) for k, (p, b) in enumerate(TILES) if b == a and (p, b) not in ONE_SIDED]
    return straight, turned


def gradient_kernel(wanted, *refs):
    tiles, blocks, outs = refs[0], refs[1 : 1 + len(ELEMENTS)], refs[1 + len(ELEMENTS) :]
    share = tiles.shape[1] // len(TILES)
    n, width = tiles.shape[2], outs[0].shape[1]

    def tile(k):
        return tiles[:, k * share : (k + 1) * share, :].reshape(NT * share, n)

    for out, a in zip(outs, wanted, strict=True):
        straight, turned = terms_of(a)
        total = None
        if straight:
            total = jnp.dot(
                jnp.concatenate([tile(k) for k, _ in straight], axis=1),
                jnp.concatenate([blocks[b][:, :width] for _, b in straight], axis=0),
                preferred_element_type=F32,
            )
        if turned:
            more = lax.dot_general(
                jnp.concatenate([tile(k) for k, _ in turned], axis=0),
                jnp.concatenate([blocks[b][:, :width] for _, b in turned], axis=0),
                (((0,), (0,)), ((), ())),
                preferred_element_type=F32,
            )
            total = more if total is None else total + more
        out[...] = total.astype(out.dtype)


def call(kernel, out_shape, flops, *operands, smem=0):
    vmem = pl.BlockSpec(memory_space=pltpu.VMEM)
    specs = [pl.BlockSpec(memory_space=pltpu.SMEM)] * smem + [vmem] * (len(operands) - smem)
    several = isinstance(out_shape, (list, tuple))
    moved = sum(x.size * x.dtype.itemsize for x in operands)
    return pl.pallas_call(
        kernel,
        out_shape=out_shape,
        in_specs=specs,
        out_specs=[vmem] * len(out_shape) if several else vmem,
        compiler_params=pltpu.CompilerParams(vmem_limit_bytes=16 * 1024 * 1024),
        cost_estimate=pl.CostEstimate(flops=flops, bytes_accessed=moved, transcendentals=0),
    )(*operands)


def on_device(student, teacher, counts):
    rows, ds = student.shape
    dt = teacher.shape[1]
    count = len(TILES)
    share = rows // NT
    z, x, s = lax.axis_index("z"), lax.axis_index("xl"), lax.axis_index("seq")

    blocks = gather(jnp.concatenate([student, teacher], axis=1))
    ends = jnp.cumsum(counts)
    sign = 1 - 2 * s
    starts = [(((z + sign * ez) % NZ) * NX + (x ^ ex)) * rows for ez, ex in ELEMENTS]
    where = jnp.stack([ends[0], ends[1], lax.axis_index(TENSOR)] + starts).astype(jnp.int32)
    r = starts[0] + jnp.arange(rows, dtype=jnp.int32)
    segment = jnp.sum((r[:, None] >= ends[None, :-1]).astype(jnp.int32), axis=1)
    index = jnp.arange(counts.shape[0], dtype=jnp.int32)
    length = jnp.sum(jnp.where(segment[:, None] == index[None, :], counts[None, :], 0), axis=1)
    scale = lax.rsqrt(length.astype(F32))
    where, scale, *blocks = lax.optimization_barrier((where, scale, *blocks))
    partial = call(
        lambda *refs: gram_kernel(
            ds, 1.0 / math.sqrt(ds * NT), 1.0 / math.sqrt(dt * NT), *refs
        ),
        jax.ShapeDtypeStruct((NT, count * share, rows), BF16),
        2 * count * rows * rows * (ds + dt),
        *blocks,
    )

    parts = lax.all_to_all(partial, TENSOR, 0, 0)
    copies = call(
        mask_kernel,
        jax.ShapeDtypeStruct(parts.shape, BF16),
        NT * count * share * rows,
        where,
        parts,
        smem=1,
    )
    tiles = lax.all_to_all(copies, TENSOR, 0, 0)

    far = [e for e, _, _ in SECOND]
    near = [0] + [e for e, _, _ in FIRST]
    block = 2 * rows * rows * ds
    given = call(
        lambda *refs: gradient_kernel(far, *refs),
        [jax.ShapeDtypeStruct((rows, ds), BF16)] * len(far),
        14 * block,
        tiles,
        student,
        *blocks[1:],
    )
    kept = call(
        lambda *refs: gradient_kernel(near, *refs),
        [jax.ShapeDtypeStruct((rows, ds), F32)] * len(near),
        18 * block,
        tiles,
        student,
        *blocks[1:],
    )
    sums = dict(zip(near, kept, strict=True))
    for (_, target, step), value in zip(SECOND, given, strict=True):
        sums[target] = sums[target] + give(value, step).astype(F32)
    for element, target, step in FIRST:
        sums[target] = sums[target] + give(sums[element].astype(BF16), step).astype(F32)

    return (sums[0] * scale[:, None]).astype(BF16)


def solution(mesh):
    split = Mesh(mesh.devices.reshape(NZ, NX, 4, 2, NSEQ), ("z", "xl", "y", "xh", "seq"))
    spec = P(("seq", "z", "xl"), TENSOR)
    return jax.shard_map(
        on_device, mesh=split, in_specs=(spec, spec, P("seq")), out_specs=spec, check_vma=False
    )
```

```python
import math

import jax
import jax.numpy as jnp
from jax import lax
from jax.experimental import pallas as pl
from jax.experimental.pallas import tpu as pltpu
from jax.sharding import Mesh, PartitionSpec as P

TENSOR = ("y", "xh")
ROW = ("z", "xl", "seq")
NZ, NX, NSEQ, NT = 16, 2, 2, 8

ELEMENTS = ((0, 0), (-2, 1), (-4, 1), (3, 0), (3, 1), (4, 0), (4, 1))
FIRST = ((1, 0, (-2, 1)), (3, 0, (3, 0)))
SECOND = ((2, 1, (-2, 0)), (6, 3, (1, 1)), (5, 3, (1, 0)), (4, 3, (0, 1)))
TILES = (
    (0, 0), (0, 1), (0, 3), (0, 4), (0, 5), (0, 6),
    (1, 2), (1, 3), (1, 4), (1, 5), (1, 6),
    (2, 3), (2, 4), (2, 5), (2, 6),
    (3, 4), (3, 5), (3, 6),
)
BATCHES = (((0, 1, 2), (3, 4, 5, 6)), ((3,), (4, 5, 6)), ((0,), (0, 1)), ((1,), (2,)))
FAR = (
    (((2,), (3, 4, 5, 6)),),
    (((0, 1), (4, 5, 6)), ((2,), (4,)), ((3,), (5, 6)), ((1,), (2,))),
)
NEAR = (
    (((0, 1), (3, 4, 5, 6)), ((0,), (0, 1)), ((1,), (2,)), ((3,), (4, 5, 6))),
    (((0, 1, 2), (3,)), ((0,), (1,))),
)
F32, BF16 = jnp.float32, jnp.bfloat16


def place(z, x, s):
    return (z % NZ * NX + x) * NSEQ + s


def moves(step, back):
    pairs = []
    for z in range(NZ):
        for x in range(NX):
            for s in range(NSEQ):
                far = place(z + (step[0] if s == 0 else -step[0]), x ^ step[1], s)
                here = place(z, x, s)
                pairs.append((here, far) if back else (far, here))
    return pairs


def fetch(block, step):
    return lax.ppermute(block, ROW, moves(step, False))


def give(block, step):
    return lax.ppermute(block, ROW, moves(step, True))


def gather(own):
    held = {0: own}
    for group in (FIRST, SECOND):
        for element, source, step in group:
            held[element] = fetch(held[source], step)
    return [held[i] for i in range(len(ELEMENTS))]


def tile_dot(left, right):
    return lax.dot_general(left, right, (((1,), (1,)), ((), ())), preferred_element_type=F32)


def gram_kernel(ds, student_scale, teacher_scale, *refs):
    blocks, out = refs[:-1], refs[-1]
    share = out.shape[1] // len(TILES)
    n = blocks[0].shape[0]

    def rows_of(elements, columns):
        return jnp.concatenate([blocks[e][:, columns] for e in elements], axis=0)

    for lefts, rights in BATCHES:
        product = (
            tile_dot(rows_of(lefts, slice(0, ds)), rows_of(rights, slice(0, ds))) * student_scale
            - tile_dot(rows_of(lefts, slice(ds, None)), rows_of(rights, slice(ds, None)))
            * teacher_scale
        )
        for i, a in enumerate(lefts):
            for j, b in enumerate(rights):
                k = TILES.index((a, b))
                tile = product[i * n : (i + 1) * n, j * n : (j + 1) * n].astype(BF16)
                out[:, k * share : (k + 1) * share, :] = tile.reshape(NT, share, n)


def mask_kernel(where_ref, parts, out):
    share = parts.shape[1] // len(TILES)
    n = parts.shape[2]
    first_end, second_end, part = where_ref[0], where_ref[1], where_ref[2]

    def segment(r):
        return (r >= first_end).astype(jnp.int32) + (r >= second_end).astype(jnp.int32)

    for k, (a, b) in enumerate(TILES):
        rows = slice(k * share, (k + 1) * share)
        total = parts[0, rows, :].astype(F32)
        for s in range(1, NT):
            total += parts[s, rows, :].astype(F32)
        r = where_ref[3 + a] + part * share + lax.broadcasted_iota(jnp.int32, (share, n), 0)
        c = where_ref[3 + b] + lax.broadcasted_iota(jnp.int32, (share, n), 1)
        kept = jnp.where(segment(r) == segment(c), total, 0.0).astype(BF16)
        for s in range(NT):
            out[s, rows, :] = kept


def gradient_kernel(wanted, straight, turned, *refs):
    tiles, blocks, outs = refs[0], refs[1 : 1 + len(ELEMENTS)], refs[1 + len(ELEMENTS) :]
    share = tiles.shape[1] // len(TILES)
    n, width = tiles.shape[2], outs[0].shape[1]

    def tile(a, b):
        k = TILES.index((a, b))
        return tiles[:, k * share : (k + 1) * share, :].reshape(NT * share, n)

    def grid_of(lefts, rights):
        return jnp.concatenate(
            [jnp.concatenate([tile(a, b) for b in rights], axis=1) for a in lefts], axis=0
        )

    def students(elements):
        return jnp.concatenate([blocks[e][:, :width] for e in elements], axis=0)

    sums = {}

    def add(elements, product):
        for i, e in enumerate(elements):
            part = product[i * n : (i + 1) * n, :]
            sums[e] = sums[e] + part if e in sums else part

    for lefts, rights in straight:
        add(lefts, jnp.dot(grid_of(lefts, rights), students(rights), preferred_element_type=F32))
    for lefts, rights in turned:
        product = lax.dot_general(
            grid_of(lefts, rights),
            students(lefts),
            (((0,), (0,)), ((), ())),
            preferred_element_type=F32,
        )
        add(rights, product)
    for out, e in zip(outs, wanted, strict=True):
        out[...] = sums[e].astype(out.dtype)


def call(kernel, out_shape, flops, *operands, smem=0):
    vmem = pl.BlockSpec(memory_space=pltpu.VMEM)
    specs = [pl.BlockSpec(memory_space=pltpu.SMEM)] * smem + [vmem] * (len(operands) - smem)
    several = isinstance(out_shape, (list, tuple))
    moved = sum(x.size * x.dtype.itemsize for x in operands)
    return pl.pallas_call(
        kernel,
        out_shape=out_shape,
        in_specs=specs,
        out_specs=[vmem] * len(out_shape) if several else vmem,
        compiler_params=pltpu.CompilerParams(vmem_limit_bytes=16 * 1024 * 1024),
        cost_estimate=pl.CostEstimate(flops=flops, bytes_accessed=moved, transcendentals=0),
    )(*operands)


def on_device(student, teacher, counts):
    rows, ds = student.shape
    dt = teacher.shape[1]
    count = len(TILES)
    share = rows // NT
    z, x, s = lax.axis_index("z"), lax.axis_index("xl"), lax.axis_index("seq")

    blocks = gather(jnp.concatenate([student, teacher], axis=1))
    ends = jnp.cumsum(counts)
    sign = 1 - 2 * s
    starts = [(((z + sign * ez) % NZ) * NX + (x ^ ex)) * rows for ez, ex in ELEMENTS]
    where = jnp.stack([ends[0], ends[1], lax.axis_index(TENSOR)] + starts).astype(jnp.int32)
    r = starts[0] + jnp.arange(rows, dtype=jnp.int32)
    segment = jnp.sum((r[:, None] >= ends[None, :-1]).astype(jnp.int32), axis=1)
    index = jnp.arange(counts.shape[0], dtype=jnp.int32)
    length = jnp.sum(jnp.where(segment[:, None] == index[None, :], counts[None, :], 0), axis=1)
    scale = lax.rsqrt(length.astype(F32))
    where, scale, *blocks = lax.optimization_barrier((where, scale, *blocks))
    partial = call(
        lambda *refs: gram_kernel(
            ds, 1.0 / math.sqrt(ds * NT), 1.0 / math.sqrt(dt * NT), *refs
        ),
        jax.ShapeDtypeStruct((NT, count * share, rows), BF16),
        2 * count * rows * rows * (ds + dt),
        *blocks,
    )

    parts = lax.all_to_all(partial, TENSOR, 0, 0)
    copies = call(
        mask_kernel,
        jax.ShapeDtypeStruct(parts.shape, BF16),
        NT * count * share * rows,
        where,
        parts,
        smem=1,
    )
    tiles = lax.all_to_all(copies, TENSOR, 0, 0)

    far = [e for e, _, _ in SECOND]
    near = [0] + [e for e, _, _ in FIRST]
    block = 2 * rows * rows * ds
    given = call(
        lambda *refs: gradient_kernel(far, *FAR, *refs),
        [jax.ShapeDtypeStruct((rows, ds), BF16)] * len(far),
        14 * block,
        tiles,
        student,
        *blocks[1:],
    )
    kept = call(
        lambda *refs: gradient_kernel(near, *NEAR, *refs),
        [jax.ShapeDtypeStruct((rows, ds), F32)] * len(near),
        18 * block,
        tiles,
        student,
        *blocks[1:],
    )
    sums = dict(zip(near, kept, strict=True))
    for (_, target, step), value in zip(SECOND, given, strict=True):
        sums[target] = sums[target] + give(value, step).astype(F32)
    for element, target, step in FIRST:
        sums[target] = sums[target] + give(sums[element].astype(BF16), step).astype(F32)

    return (sums[0] * scale[:, None]).astype(BF16)


def solution(mesh):
    split = Mesh(mesh.devices.reshape(NZ, NX, 4, 2, NSEQ), ("z", "xl", "y", "xh", "seq"))
    spec = P(("seq", "z", "xl"), TENSOR)
    return jax.shard_map(
        on_device, mesh=split, in_specs=(spec, spec, P("seq")), out_specs=spec, check_vma=False
    )
```

```python
import math

import jax
import jax.numpy as jnp
from jax import lax
from jax.experimental import pallas as pl
from jax.experimental.pallas import tpu as pltpu
from jax.sharding import Mesh, PartitionSpec as P

TENSOR = ("y", "xh")
ROW = ("z", "xl", "seq")
NZ, NX, NSEQ, NT = 16, 2, 2, 8

ELEMENTS = ((0, 0), (-2, 1), (-4, 1), (3, 0), (3, 1), (4, 0), (4, 1))
FIRST = ((1, 0, (-2, 1)), (3, 0, (3, 0)))
SECOND = ((2, 1, (-2, 0)), (6, 3, (1, 1)), (5, 3, (1, 0)), (4, 3, (0, 1)))
TILES = (
    (0, 0), (0, 1), (0, 3), (0, 4), (0, 5), (0, 6),
    (1, 2), (1, 3), (1, 4), (1, 5), (1, 6),
    (2, 3), (2, 4), (2, 5), (2, 6),
    (3, 4), (3, 5), (3, 6),
)
BATCHES = (((0, 1, 2), (3, 4, 5, 6)), ((3,), (4, 5, 6)), ((0,), (0, 1)), ((1,), (2,)))
ONE_SIDED = ((0, 0), (2, 5), (2, 6), (3, 4))
F32, BF16 = jnp.float32, jnp.bfloat16


def place(z, x, s):
    return (z % NZ * NX + x) * NSEQ + s


def moves(step, back):
    pairs = []
    for z in range(NZ):
        for x in range(NX):
            for s in range(NSEQ):
                far = place(z + (step[0] if s == 0 else -step[0]), x ^ step[1], s)
                here = place(z, x, s)
                pairs.append((here, far) if back else (far, here))
    return pairs


def fetch(block, step):
    return lax.ppermute(block, ROW, moves(step, False))


def give(block, step):
    return lax.ppermute(block, ROW, moves(step, True))


def gather(own):
    held = {0: own}
    for group in (FIRST, SECOND):
        for element, source, step in group:
            held[element] = fetch(held[source], step)
    return [held[i] for i in range(len(ELEMENTS))]


def tile_dot(left, right):
    return lax.dot_general(left, right, (((1,), (1,)), ((), ())), preferred_element_type=F32)


def gram_kernel(ds, student_scale, teacher_scale, *refs):
    blocks, out = refs[:-1], refs[-1]
    share = out.shape[1] // len(TILES)
    n = blocks[0].shape[0]

    def rows_of(elements, columns):
        return jnp.concatenate([blocks[e][:, columns] for e in elements], axis=0)

    for lefts, rights in BATCHES:
        product = (
            tile_dot(rows_of(lefts, slice(0, ds)), rows_of(rights, slice(0, ds))) * student_scale
            - tile_dot(rows_of(lefts, slice(ds, None)), rows_of(rights, slice(ds, None)))
            * teacher_scale
        )
        for i, a in enumerate(lefts):
            for j, b in enumerate(rights):
                k = TILES.index((a, b))
                tile = product[i * n : (i + 1) * n, j * n : (j + 1) * n].astype(BF16)
                out[:, k * share : (k + 1) * share, :] = tile.reshape(NT, share, n)


def mask_kernel(where_ref, parts, out):
    share = parts.shape[1] // len(TILES)
    n = parts.shape[2]
    first_end, second_end, part = where_ref[0], where_ref[1], where_ref[2]

    def segment(r):
        return (r >= first_end).astype(jnp.int32) + (r >= second_end).astype(jnp.int32)

    for k, (a, b) in enumerate(TILES):
        rows = slice(k * share, (k + 1) * share)
        total = parts[0, rows, :].astype(F32)
        for s in range(1, NT):
            total += parts[s, rows, :].astype(F32)
        r = where_ref[3 + a] + part * share + lax.broadcasted_iota(jnp.int32, (share, n), 0)
        c = where_ref[3 + b] + lax.broadcasted_iota(jnp.int32, (share, n), 1)
        kept = jnp.where(segment(r) == segment(c), total, 0.0).astype(BF16)
        for s in range(NT):
            out[s, rows, :] = kept


def terms_of(a):
    straight = [(k, b) for k, (p, b) in enumerate(TILES) if p == a]
    turned = [(k, p) for k, (p, b) in enumerate(TILES) if b == a and (p, b) not in ONE_SIDED]
    return straight, turned


def gradient_kernel(wanted, *refs):
    tiles, blocks, outs = refs[0], refs[1 : 1 + len(ELEMENTS)], refs[1 + len(ELEMENTS) :]
    share = tiles.shape[1] // len(TILES)
    n, width = tiles.shape[2], outs[0].shape[1]

    def tile(k):
        return tiles[:, k * share : (k + 1) * share, :].reshape(NT * share, n)

    for out, a in zip(outs, wanted, strict=True):
        straight, turned = terms_of(a)
        total = None
        if straight:
            total = jnp.dot(
                jnp.concatenate([tile(k) for k, _ in straight], axis=1),
                jnp.concatenate([blocks[b][:, :width] for _, b in straight], axis=0),
                preferred_element_type=F32,
            )
        if turned:
            more = lax.dot_general(
                jnp.concatenate([tile(k) for k, _ in turned], axis=0),
                jnp.concatenate([blocks[b][:, :width] for _, b in turned], axis=0),
                (((0,), (0,)), ((), ())),
                preferred_element_type=F32,
            )
            total = more if total is None else total + more
        out[...] = total.astype(out.dtype)


def call(kernel, out_shape, flops, *operands, smem=0):
    vmem = pl.BlockSpec(memory_space=pltpu.VMEM)
    specs = [pl.BlockSpec(memory_space=pltpu.SMEM)] * smem + [vmem] * (len(operands) - smem)
    several = isinstance(out_shape, (list, tuple))
    moved = sum(x.size * x.dtype.itemsize for x in operands)
    return pl.pallas_call(
        kernel,
        out_shape=out_shape,
        in_specs=specs,
        out_specs=[vmem] * len(out_shape) if several else vmem,
        compiler_params=pltpu.CompilerParams(vmem_limit_bytes=16 * 1024 * 1024),
        cost_estimate=pl.CostEstimate(flops=flops, bytes_accessed=moved, transcendentals=0),
    )(*operands)


def on_device(student, teacher, counts):
    rows, ds = student.shape
    dt = teacher.shape[1]
    count = len(TILES)
    share = rows // NT
    z, x, s = lax.axis_index("z"), lax.axis_index("xl"), lax.axis_index("seq")

    blocks = gather(jnp.concatenate([student, teacher], axis=1))
    ends = jnp.cumsum(counts)
    sign = 1 - 2 * s
    starts = [(((z + sign * ez) % NZ) * NX + (x ^ ex)) * rows for ez, ex in ELEMENTS]
    where = jnp.stack([ends[0], ends[1], lax.axis_index(TENSOR)] + starts).astype(jnp.int32)
    r = starts[0] + jnp.arange(rows, dtype=jnp.int32)
    segment = jnp.sum((r[:, None] >= ends[None, :-1]).astype(jnp.int32), axis=1)
    index = jnp.arange(counts.shape[0], dtype=jnp.int32)
    length = jnp.sum(jnp.where(segment[:, None] == index[None, :], counts[None, :], 0), axis=1)
    scale = lax.rsqrt(length.astype(F32))
    where, scale, *blocks = lax.optimization_barrier((where, scale, *blocks))
    partial = call(
        lambda *refs: gram_kernel(
            ds, 1.0 / math.sqrt(ds * NT), 1.0 / math.sqrt(dt * NT), *refs
        ),
        jax.ShapeDtypeStruct((NT, count * share, rows), BF16),
        2 * count * rows * rows * (ds + dt),
        *blocks,
    )

    parts = lax.all_to_all(partial, TENSOR, 0, 0)
    copies = call(
        mask_kernel,
        jax.ShapeDtypeStruct(parts.shape, BF16),
        NT * count * share * rows,
        where,
        parts,
        smem=1,
    )
    tiles = lax.all_to_all(copies, TENSOR, 0, 0)

    far = [e for e, _, _ in SECOND]
    near = [0] + [e for e, _, _ in FIRST]
    block = 2 * rows * rows * ds
    both = call(
        lambda *refs: gradient_kernel(far + near, *refs),
        [jax.ShapeDtypeStruct((rows, ds), BF16)] * len(far)
        + [jax.ShapeDtypeStruct((rows, ds), F32)] * len(near),
        32 * block,
        tiles,
        student,
        *blocks[1:],
    )
    given, kept = both[: len(far)], both[len(far) :]
    sums = dict(zip(near, kept, strict=True))
    for (_, target, step), value in zip(SECOND, given, strict=True):
        sums[target] = sums[target] + give(value, step).astype(F32)
    for element, target, step in FIRST:
        sums[target] = sums[target] + give(sums[element].astype(BF16), step).astype(F32)

    return (sums[0] * scale[:, None]).astype(BF16)


def solution(mesh):
    split = Mesh(mesh.devices.reshape(NZ, NX, 4, 2, NSEQ), ("z", "xl", "y", "xh", "seq"))
    spec = P(("seq", "z", "xl"), TENSOR)
    return jax.shard_map(
        on_device, mesh=split, in_specs=(spec, spec, P("seq")), out_specs=spec, check_vma=False
    )
```

```python
import math

import jax
import jax.numpy as jnp
from jax import lax
from jax.experimental import pallas as pl
from jax.experimental.pallas import tpu as pltpu
from jax.sharding import Mesh, PartitionSpec as P

TENSOR = ("y", "xh")
ROW = ("z", "xl", "seq")
NZ, NX, NSEQ, NT = 16, 2, 2, 8

ELEMENTS = ((0, 0), (-2, 1), (-4, 1), (3, 0), (3, 1), (4, 0), (4, 1))
FIRST = ((1, 0, (-2, 1)), (3, 0, (3, 0)))
SECOND = ((2, 1, (-2, 0)), (6, 3, (1, 1)), (5, 3, (1, 0)), (4, 3, (0, 1)))
TILES = (
    (0, 0), (0, 1), (0, 3), (0, 4), (0, 5), (0, 6),
    (1, 2), (1, 3), (1, 4), (1, 5), (1, 6),
    (2, 3), (2, 4), (2, 5), (2, 6),
    (3, 4), (3, 5), (3, 6),
)
BATCHES = (((0, 1, 2), (3, 4, 5, 6)), ((3,), (4, 5, 6)), ((0,), (0, 1)), ((1,), (2,)))
STRAIGHT = (((0, 1, 2), (3, 4, 5, 6)), ((0,), (0, 1)), ((1,), (2,)), ((3,), (4, 5, 6)))
TURNED = (((0, 1), (3, 4, 5, 6)), ((2,), (3, 4)), ((0,), (1,)), ((1,), (2,)), ((3,), (5, 6)))
F32, BF16 = jnp.float32, jnp.bfloat16


def place(z, x, s):
    return (z % NZ * NX + x) * NSEQ + s


def moves(step, back):
    pairs = []
    for z in range(NZ):
        for x in range(NX):
            for s in range(NSEQ):
                far = place(z + (step[0] if s == 0 else -step[0]), x ^ step[1], s)
                here = place(z, x, s)
                pairs.append((here, far) if back else (far, here))
    return pairs


def fetch(block, step):
    return lax.ppermute(block, ROW, moves(step, False))


def give(block, step):
    return lax.ppermute(block, ROW, moves(step, True))


def gather(own):
    held = {0: own}
    for group in (FIRST, SECOND):
        for element, source, step in group:
            held[element] = fetch(held[source], step)
    return [held[i] for i in range(len(ELEMENTS))]


def tile_dot(left, right):
    return lax.dot_general(left, right, (((1,), (1,)), ((), ())), preferred_element_type=F32)


def gram_kernel(ds, student_scale, teacher_scale, *refs):
    blocks, out = refs[:-1], refs[-1]
    share = out.shape[1] // len(TILES)
    n = blocks[0].shape[0]

    def rows_of(elements, columns):
        return jnp.concatenate([blocks[e][:, columns] for e in elements], axis=0)

    for lefts, rights in BATCHES:
        product = (
            tile_dot(rows_of(lefts, slice(0, ds)), rows_of(rights, slice(0, ds))) * student_scale
            - tile_dot(rows_of(lefts, slice(ds, None)), rows_of(rights, slice(ds, None)))
            * teacher_scale
        )
        for i, a in enumerate(lefts):
            for j, b in enumerate(rights):
                k = TILES.index((a, b))
                tile = product[i * n : (i + 1) * n, j * n : (j + 1) * n].astype(BF16)
                out[:, k * share : (k + 1) * share, :] = tile.reshape(NT, share, n)


def mask_kernel(where_ref, parts, out):
    share = parts.shape[1] // len(TILES)
    n = parts.shape[2]
    first_end, second_end, part = where_ref[0], where_ref[1], where_ref[2]

    def segment(r):
        return (r >= first_end).astype(jnp.int32) + (r >= second_end).astype(jnp.int32)

    for k, (a, b) in enumerate(TILES):
        rows = slice(k * share, (k + 1) * share)
        total = parts[0, rows, :].astype(F32)
        for s in range(1, NT):
            total += parts[s, rows, :].astype(F32)
        r = where_ref[3 + a] + part * share + lax.broadcasted_iota(jnp.int32, (share, n), 0)
        c = where_ref[3 + b] + lax.broadcasted_iota(jnp.int32, (share, n), 1)
        kept = jnp.where(segment(r) == segment(c), total, 0.0).astype(BF16)
        for s in range(NT):
            out[s, rows, :] = kept


def gradient_kernel(wanted, straight, turned, *refs):
    tiles, blocks, outs = refs[0], refs[1 : 1 + len(ELEMENTS)], refs[1 + len(ELEMENTS) :]
    share = tiles.shape[1] // len(TILES)
    n, width = tiles.shape[2], outs[0].shape[1]

    def tile(a, b):
        k = TILES.index((a, b))
        return tiles[:, k * share : (k + 1) * share, :].reshape(NT * share, n)

    def grid_of(lefts, rights):
        return jnp.concatenate(
            [jnp.concatenate([tile(a, b) for b in rights], axis=1) for a in lefts], axis=0
        )

    def students(elements):
        return jnp.concatenate([blocks[e][:, :width] for e in elements], axis=0)

    sums = {}

    def add(elements, product):
        for i, e in enumerate(elements):
            part = product[i * n : (i + 1) * n, :]
            sums[e] = sums[e] + part if e in sums else part

    for lefts, rights in straight:
        add(lefts, jnp.dot(grid_of(lefts, rights), students(rights), preferred_element_type=F32))
    for lefts, rights in turned:
        product = lax.dot_general(
            grid_of(lefts, rights),
            students(lefts),
            (((0,), (0,)), ((), ())),
            preferred_element_type=F32,
        )
        add(rights, product)
    for out, e in zip(outs, wanted, strict=True):
        out[...] = sums[e].astype(out.dtype)


def call(kernel, out_shape, flops, *operands, smem=0):
    vmem = pl.BlockSpec(memory_space=pltpu.VMEM)
    specs = [pl.BlockSpec(memory_space=pltpu.SMEM)] * smem + [vmem] * (len(operands) - smem)
    several = isinstance(out_shape, (list, tuple))
    moved = sum(x.size * x.dtype.itemsize for x in operands)
    return pl.pallas_call(
        kernel,
        out_shape=out_shape,
        in_specs=specs,
        out_specs=[vmem] * len(out_shape) if several else vmem,
        compiler_params=pltpu.CompilerParams(vmem_limit_bytes=16 * 1024 * 1024),
        cost_estimate=pl.CostEstimate(flops=flops, bytes_accessed=moved, transcendentals=0),
    )(*operands)


def on_device(student, teacher, counts):
    rows, ds = student.shape
    dt = teacher.shape[1]
    count = len(TILES)
    share = rows // NT
    z, x, s = lax.axis_index("z"), lax.axis_index("xl"), lax.axis_index("seq")

    blocks = gather(jnp.concatenate([student, teacher], axis=1))
    ends = jnp.cumsum(counts)
    sign = 1 - 2 * s
    starts = [(((z + sign * ez) % NZ) * NX + (x ^ ex)) * rows for ez, ex in ELEMENTS]
    where = jnp.stack([ends[0], ends[1], lax.axis_index(TENSOR)] + starts).astype(jnp.int32)
    r = starts[0] + jnp.arange(rows, dtype=jnp.int32)
    segment = jnp.sum((r[:, None] >= ends[None, :-1]).astype(jnp.int32), axis=1)
    index = jnp.arange(counts.shape[0], dtype=jnp.int32)
    length = jnp.sum(jnp.where(segment[:, None] == index[None, :], counts[None, :], 0), axis=1)
    scale = lax.rsqrt(length.astype(F32))
    where, scale, *blocks = lax.optimization_barrier((where, scale, *blocks))
    partial = call(
        lambda *refs: gram_kernel(
            ds, 1.0 / math.sqrt(ds * NT), 1.0 / math.sqrt(dt * NT), *refs
        ),
        jax.ShapeDtypeStruct((NT, count * share, rows), BF16),
        2 * count * rows * rows * (ds + dt),
        *blocks,
    )

    parts = lax.all_to_all(partial, TENSOR, 0, 0)
    copies = call(
        mask_kernel,
        jax.ShapeDtypeStruct(parts.shape, BF16),
        NT * count * share * rows,
        where,
        parts,
        smem=1,
    )
    tiles = lax.all_to_all(copies, TENSOR, 0, 0)

    far = [e for e, _, _ in SECOND]
    near = [0] + [e for e, _, _ in FIRST]
    block = 2 * rows * rows * ds
    both = call(
        lambda *refs: gradient_kernel(far + near, STRAIGHT, TURNED, *refs),
        [jax.ShapeDtypeStruct((rows, ds), BF16)] * len(far)
        + [jax.ShapeDtypeStruct((rows, ds), F32)] * len(near),
        32 * block,
        tiles,
        student,
        *blocks[1:],
    )
    given, kept = both[: len(far)], both[len(far) :]
    sums = dict(zip(near, kept, strict=True))
    for (_, target, step), value in zip(SECOND, given, strict=True):
        sums[target] = sums[target] + give(value, step).astype(F32)
    for element, target, step in FIRST:
        sums[target] = sums[target] + give(sums[element].astype(BF16), step).astype(F32)

    return (sums[0] * scale[:, None]).astype(BF16)


def solution(mesh):
    split = Mesh(mesh.devices.reshape(NZ, NX, 4, 2, NSEQ), ("z", "xl", "y", "xh", "seq"))
    spec = P(("seq", "z", "xl"), TENSOR)
    return jax.shard_map(
        on_device, mesh=split, in_specs=(spec, spec, P("seq")), out_specs=spec, check_vma=False
    )
```
